32 devices in a mesh: grp: 4 (over x, core), dev: 8 (over z, y).
Axes of the slice: x: 2, y: 2, z: 4, core: 2. Of those that a mesh axis runs over, the one named last changes fastest.
Arguments:
- matrix_slab: float32 [32, 131072], P(None, ('grp', 'dev')), may hold values from -6 to 6
- sign_flips: int32 [131072], P(('grp', 'dev')), may hold values from 0 to 1
- sample_offset: int32 [512], P(('grp', 'dev')), may hold values from 0 to 4095, as said below
Outputs:
- transformed: float32 [32, 131072], P(None, ('grp', 'dev'))
- sketch: float32 [32, 512], P(None, ('grp', 'dev'))
- gram_matrix: float32 [32, 32], replicated
The draws below stay inside these ranges and needn't reach their ends.
Inputs may be any that keep to these rules, and one draw needn't show every extreme that they name: Entry k selects row (k // 16) * 4096 + sample_offset[k] of the transform; rows may repeat.
All inputs are finite; a program needn't handle non-finite values.
Results may differ from the reference program's by a relative error of at most 0.00011.
Values sent between devices are 32-bit elements; how exact they have to be, the bound alone decides.
No kernel may reach another device: no remote copies, remote signals or barrier semaphores. Data moves between devices by JAX's collectives and lax.ppermute only.
A program may use at most 64 MiB of HBM per device.

```python
import math
import jax
import jax.numpy as jnp
from jax import lax

COLS = 32
ROWS_DEV = 4096
SAMP_DEV = 16
ROWS = 131072
SAMPLES = 512


def draw_sample_offset(key, part):
    key = jax.random.fold_in(key, 11)
    picked = jax.random.randint(key, (SAMPLES,), 0, ROWS_DEV, dtype=jnp.int32)
    picked = picked.at[0].set(0)
    picked = picked.at[SAMPLES - 1].set(ROWS_DEV - 1)
    return picked


def plant(values, key, smallest, largest):
    shape = values.shape
    place = [jax.random.randint(jax.random.fold_in(key, axis), (), 0, shape[axis]) for axis in range(len(shape))]
    values = values.at[tuple(place)].set(smallest)
    longest = shape.index(max(shape))
    place[longest] = (place[longest] + 1) % shape[longest]
    return values.at[tuple(place)].set(largest)


def shard_levels(key, dims, pieces, low, high):
    gain, own = 1.0, jax.random.fold_in(key, 6)
    for dim, shards_of in pieces:
        heights = jnp.exp(jax.random.uniform(jax.random.fold_in(own, dim), (shards_of,), jnp.float32, low / len(pieces), high / len(pieces)))
        gain = gain * jnp.repeat(heights, dims[dim] // shards_of).reshape([-1 if axis == dim else 1 for axis in range(len(dims))])
    return gain


def centred(stream_key, shape, scale, most, pieces=(), held_as=jnp.bfloat16):
    drawn = jax.random.normal(stream_key, shape, jnp.float32) * scale
    if len(pieces) > 0:
        drawn = shard_levels(stream_key, shape, pieces, -0.22, 0.18) * drawn
    return jnp.clip(drawn, min=-most, max=most).astype(held_as)


def setup_inputs(seed: int = 0) -> dict:
    arg_keys = jax.random.split(jax.random.key(seed), 4)
    matrix_slab = centred(arg_keys[0], (COLS, ROWS), 1.0, 6.0, ((1, 32),), jnp.float32)
    sign_flips = plant(jax.random.randint(arg_keys[1], (ROWS,), 0, 2), jax.random.fold_in(arg_keys[1], 1), 0, 1).astype(jnp.int32)
    sample_offset = draw_sample_offset(jax.random.fold_in(arg_keys[3], 71), 0)
    return {"matrix_slab": matrix_slab, "sign_flips": sign_flips, "sample_offset": sample_offset}


def hadamard_table(order):
    numbers = jnp.arange(order, dtype=jnp.int32)
    common_bits = numbers[:, None] & numbers[None, :]
    parity = jnp.zeros((order, order), dtype=jnp.int32)
    for position in range(max(order.bit_length() - 1, 0)):
        parity = parity + (common_bits >> position & 1)
    return (1 - 2 * (parity % 2)).astype(jnp.float32)

def split_sizes(length):
    factors = []
    remain = length
    while remain > 1:
        factor = min(128, remain)
        factors.append(factor)
        remain = remain // factor
    return factors

def mix_last(values, length):
    leading = values.shape[:-1]
    factors = split_sizes(length)
    if len(factors) == 0:
        return values
    shaped = values.reshape(leading + tuple(factors))
    letters = 'abcdefghij'
    total = len(leading) + len(factors)
    source = letters[:total]
    for position in range(len(factors)):
        axis_at = len(leading) + position
        target = source[:axis_at] + 'z' + source[axis_at + 1:]
        shaped = jnp.einsum(source + ',z' + source[axis_at] + '->' + target, shaped, hadamard_table(factors[position]), precision=lax.Precision.HIGHEST)
    return shaped.reshape(values.shape)

def reference(matrix_slab, sign_flips, sample_offset):
    signs = (1 - 2 * sign_flips).astype(jnp.float32)
    signed = matrix_slab * signs[None, :]
    transformed = mix_last(signed, ROWS) * jnp.float32(1.0 / math.sqrt(ROWS))
    blocks = (jnp.arange(SAMPLES, dtype=jnp.int32) // SAMP_DEV).astype(jnp.int32)
    chosen = (blocks * ROWS_DEV + sample_offset).astype(jnp.int32)
    sketch = jnp.take(transformed, chosen, axis=1)
    gram_matrix = jnp.dot(sketch, sketch.T, precision=lax.Precision.HIGHEST, preferred_element_type=jnp.float32) / jnp.float32(SAMPLES)
    return (transformed, sketch, gram_matrix)
```

```python
import functools
import math

import jax
import jax.numpy as jnp
from jax import lax
from jax.experimental import pallas as pl
from jax.experimental.pallas import tpu as pltpu
from jax.sharding import PartitionSpec as P

AXES = ("grp", "dev")
LANES = 128
ROWS = 8
IN_VMEM = pl.BlockSpec(memory_space=pltpu.VMEM)
IN_SMEM = pl.BlockSpec(memory_space=pltpu.SMEM)
IN_HBM = pl.BlockSpec(memory_space=pltpu.HBM)


def call(body, outputs, in_specs, args, out_specs=None, scratch=()):
    return pl.pallas_call(
        body,
        out_shape=outputs,
        in_specs=in_specs,
        out_specs=jax.tree.map(lambda _: IN_VMEM, outputs) if out_specs is None else out_specs,
        scratch_shapes=scratch,
        compiler_params=pltpu.CompilerParams(vmem_limit_bytes=24 * 1024 * 1024),
    )(*args)


def block(rows, width, dtype=jnp.float32):
    return jax.ShapeDtypeStruct((rows, width), dtype)


def lanes_of(index):
    return slice(index * LANES, (index + 1) * LANES)


def exchange(array, core, masks):
    count = lax.axis_size(AXES)
    route = [(place, place ^ masks[0 if place & core == 0 else 1]) for place in range(count)]
    return lax.ppermute(array, AXES, route)


def chosen_mask(place, core, masks):
    return jnp.where(place & core == 0, masks[0], masks[1])


def combine(current, partner, core, masks):
    place = lax.axis_index(AXES)
    lower = place & chosen_mask(place, core, masks) == 0
    return jnp.where(lower, current + partner, partner - current)


def three_parts(values):
    high = values.astype(jnp.bfloat16)
    rest = values - high.astype(jnp.float32)
    middle = rest.astype(jnp.bfloat16)
    low = (rest - middle.astype(jnp.float32)).astype(jnp.bfloat16)
    return high, middle, low


def exact_dot(values, table):
    total = None
    for piece in three_parts(values):
        product = jnp.dot(piece, table, preferred_element_type=jnp.float32)
        total = product if total is None else total + product
    return total


def mix(parts):
    left = lax.broadcasted_iota(jnp.int32, (LANES, LANES), 0)
    right = lax.broadcasted_iota(jnp.int32, (LANES, LANES), 1)
    parity = left & right
    for shift in (4, 2, 1):
        parity = parity ^ (parity >> shift)
    table = (1 - 2 * (parity & 1)).astype(jnp.float32).astype(jnp.bfloat16)
    parts = list(parts)
    span = 1
    while span < len(parts):
        for index in range(len(parts)):
            if index & span == 0:
                first, second = parts[index], parts[index | span]
                parts[index], parts[index | span] = first + second, first - second
        span *= 2
    total = exact_dot(jnp.concatenate(parts, axis=0), table)
    rows = parts[0].shape[0]
    return [total[index * rows : (index + 1) * rows] for index in range(len(parts))]


def own_kernel(scaling, core, place_ref, slab_ref, flips_ref, out_ref):
    columns = out_ref.shape[0]
    top = jnp.where(place_ref[0] & core == 0, 0, columns)
    for index in range(flips_ref.shape[0]):
        sign = jnp.where(flips_ref[index : index + 1, :] == 0, scaling, -scaling)
        rows = pl.ds(pl.multiple_of(top, ROWS), columns)
        out_ref[:, lanes_of(index)] = slab_ref[rows, lanes_of(index)] * sign


def split_kernel(scaling, core, place_ref, own_ref, other_ref, flips_ref, offset_ref, other_offset_ref, *out_refs):
    chunk_refs, tile_ref = out_refs[:-1], out_refs[-1]
    columns = own_ref.shape[0]
    on_first = place_ref[0] & core == 0
    top = jnp.where(on_first, 0, columns)
    turn = jnp.where(on_first, 1.0, -1.0)
    for index in range(flips_ref.shape[0]):
        here = lanes_of(index)
        sign = jnp.where(flips_ref[index : index + 1, :] == 0, scaling, -scaling)
        for number, chunk_ref in enumerate(chunk_refs):
            own = own_ref[number * ROWS : (number + 1) * ROWS, here]
            other = other_ref[pl.ds(pl.multiple_of(top + number * ROWS, ROWS), ROWS), here] * sign
            chunk_ref[:ROWS, here] = own + other
            chunk_ref[ROWS:, here] = (own - other) * turn
    samples = offset_ref.shape[1]
    first = jnp.where(on_first, offset_ref[...], other_offset_ref[...])
    second = jnp.where(on_first, other_offset_ref[...], offset_ref[...])
    tile = jnp.concatenate([first, second] * (LANES // (2 * samples)), axis=1)
    tile_ref[...] = jnp.broadcast_to(tile.astype(jnp.float32), tile_ref.shape)


def mix_kernel(core, masks, place_ref, own_ref, other_ref, tile_ref, out_ref):
    slices = own_ref.shape[1] // LANES
    factor = jnp.where(place_ref[0] & chosen_mask(place_ref[0], core, masks) == 0, 1.0, -1.0)
    parts = [
        own_ref[:, lanes_of(index)] * factor + other_ref[:, lanes_of(index)] for index in range(slices)
    ]
    for index, part in enumerate(mix(parts)):
        out_ref[:, lanes_of(index)] = part
    for row in range(0, own_ref.shape[0], ROWS):
        out_ref[row : row + ROWS, lanes_of(slices)] = tile_ref[...]


def second_kernel(core, masks, place_ref, own_ref, other_ref, out_ref):
    factor = jnp.where(place_ref[0] & chosen_mask(place_ref[0], core, masks) == 0, 1.0, -1.0)
    width = out_ref.shape[1]
    out_ref[...] = own_ref[:, :width] * factor + other_ref[:, :width]


def pick_kernel(core, all_masks, place_ref, tile_ref, *refs):
    count = len(all_masks)
    chunk_refs, other_refs, out_ref = refs[:count], refs[count:-1], refs[-1]
    samples = out_ref.shape[1] * 2
    lane = lax.broadcasted_iota(jnp.int32, (1, LANES), 1)
    place_in = lax.broadcasted_iota(jnp.int32, (LANES, LANES), 0)
    own_chip = lane < 2 * samples
    shares = []
    for masks, chunk_ref, other_ref in zip(all_masks, chunk_refs, other_refs):
        partner = other_ref[0:1, other_ref.shape[1] - LANES :]
        offsets = jnp.where(own_chip, tile_ref[0:1, :], partner).astype(jnp.int32)
        chosen = jnp.where(place_in == offsets % LANES, 1.0, 0.0).astype(jnp.bfloat16)
        side = jnp.where(place_ref[0] & chosen_mask(place_ref[0], core, masks) == 0, 1.0, -1.0)
        slices = chunk_ref.shape[1] // LANES
        rows = chunk_ref.shape[0]
        stacked = jnp.concatenate([chunk_ref[:, lanes_of(index)] for index in range(slices)], axis=0)
        found = exact_dot(stacked, chosen)
        share = jnp.zeros((rows, LANES), jnp.float32)
        for index in range(slices):
            share = jnp.where(offsets // LANES == index, found[index * rows : (index + 1) * rows], share)
        share = jnp.where(lane // samples % 2 == 0, share[:ROWS], share[ROWS:])
        shares.append(share * jnp.where(own_chip, side, 1.0))
    turned = jnp.concatenate(shares, axis=0).T
    half = samples // 2
    starts = [kind * samples + part * half for part in range(2) for kind in range(4)]
    tile = jnp.concatenate([turned[start : start + half] for start in starts], axis=1)
    for place in range(out_ref.shape[0]):
        out_ref[place] = tile


def gram_kernel(core, all_masks, place_ref, shares_ref, gram_ref, sketch_ref):
    count, rows, _ = shares_ref.shape
    columns = gram_ref.shape[0]
    width = columns // 2
    lane = lax.broadcasted_iota(jnp.int32, (rows, LANES), 1)
    number = lane % width // ROWS

    def of_core(place, second):
        others = shares_ref[place ^ all_masks[0][second]]
        for chunk in range(1, len(all_masks)):
            others = jnp.where(number == chunk, shares_ref[place ^ all_masks[chunk][second]], others)
        return shares_ref[place] + pltpu.roll(others, LANES - columns, 1)

    def of_chip(place):
        second = pltpu.roll(of_core(place | core, 1), columns, 1)
        return jnp.where(lane % (2 * columns) < columns, of_core(place, 0), second)

    chips = [place for place in range(count) if place & core == 0]
    stacked = jnp.concatenate([of_chip(place) for place in chips], axis=0)
    product = functools.partial(
        lax.dot_general, precision=lax.Precision.HIGHEST, preferred_element_type=jnp.float32
    )
    gram = product(stacked, stacked, (((0,), (0,)), ((), ())))
    down = lax.broadcasted_iota(jnp.int32, (LANES, LANES), 0)
    across = lax.broadcasted_iota(jnp.int32, (LANES, LANES), 1)

    def sample_of(spot):
        return spot // (2 * columns) * 2 + spot // width % 2

    gram = jnp.where(sample_of(down) == sample_of(across), gram, 0.0)
    spot = lax.broadcasted_iota(jnp.int32, (LANES, columns), 0)
    column = lax.broadcasted_iota(jnp.int32, (LANES, columns), 1)
    column_of = spot // columns % 2 * width + spot % width
    fold = jnp.where(column_of == column, 1.0, 0.0)
    gram = product(product(gram, fold, (((1,), (0,)), ((), ()))), fold, (((0,), (0,)), ((), ())))
    gram_ref[...] = gram * (1.0 / (count * 2 * rows))
    chip = place_ref[0] & ~core
    own = of_chip(chip)
    on_second = jnp.where(place_ref[0] & core == 0, 0, 1)
    for part in range(2):
        wanted = (column_of == column) & (sample_of(spot) == part * 2 + on_second)
        sketch_ref[part * rows : (part + 1) * rows] = exact_dot(
            own, jnp.where(wanted, 1.0, 0.0).astype(jnp.bfloat16)
        )


def last_kernel(core, masks, place_ref, own_ref, other_ref, keep_ref, send_ref):
    on_first = place_ref[0] & core == 0
    factor = jnp.where(place_ref[0] & chosen_mask(place_ref[0], core, masks) == 0, 1.0, -1.0)
    for out_ref, top in ((keep_ref, jnp.where(on_first, 0, ROWS)), (send_ref, jnp.where(on_first, ROWS, 0))):
        rows = pl.ds(pl.multiple_of(top, ROWS), ROWS)
        out_ref[...] = own_ref[rows, :] * factor + other_ref[rows, :]


def join_kernel(core, place_ref, *refs):
    block_refs, (whole_ref, sems) = refs[:-2], refs[-2:]
    on_first = place_ref[0] & core == 0
    half = whole_ref.shape[0] // 2
    tops = []
    for kept in (True, False):
        base = jnp.where(on_first, 0, half) if kept else jnp.where(on_first, half, 0)
        tops += [base + row for row in range(0, half, ROWS)]
    copies = [
        pltpu.make_async_copy(
            block_ref, whole_ref.at[pl.ds(pl.multiple_of(top, ROWS), ROWS)], sems.at[number]
        )
        for number, (block_ref, top) in enumerate(zip(block_refs, tops))
    ]
    for copy in copies:
        copy.start()
    for copy in copies:
        copy.wait()


def local_any(matrix_slab, sign_flips, sample_offset):
    columns, local_rows = matrix_slab.shape
    count = lax.axis_size(AXES)
    samples = sample_offset.shape[0]
    numbers = jnp.arange(local_rows, dtype=jnp.int32)

    def table(order):
        common = numbers[:order, None] & numbers[None, :order]
        return (1 - 2 * (lax.population_count(common) & 1)).astype(jnp.float32)

    signs = (1 - 2 * sign_flips).astype(jnp.float32) * jnp.float32(1.0 / math.sqrt(local_rows * count))
    outer = local_rows // LANES
    shaped = (matrix_slab * signs[None, :]).reshape(columns, outer, LANES)
    shaped = jnp.einsum("cak,kz->caz", shaped, table(LANES), precision=lax.Precision.HIGHEST)
    shaped = jnp.einsum("cak,az->czk", shaped, table(outer), precision=lax.Precision.HIGHEST)
    current = shaped.reshape(columns, local_rows)
    for bit in range(count.bit_length() - 1):
        masks = (1 << bit, 1 << bit)
        current = combine(current, exchange(current, 1, masks), 1, masks)
    sketch = jnp.take(current, sample_offset, axis=1)
    gram = jnp.dot(sketch, sketch.T, precision=lax.Precision.HIGHEST)
    return (current, sketch, lax.psum(gram, AXES) / jnp.float32(samples * count))


def local(matrix_slab, sign_flips, sample_offset):
    columns, local_rows = matrix_slab.shape
    grp_bits = lax.axis_size("grp").bit_length() - 1
    dev_bits = lax.axis_size("dev").bit_length() - 1
    count = lax.axis_size(AXES)
    samples = sample_offset.shape[0]
    if (grp_bits, dev_bits, columns, samples) != (2, 3, 4 * ROWS, 2 * ROWS):
        return local_any(matrix_slab, sign_flips, sample_offset)
    place = lax.axis_index(AXES).astype(jnp.int32).reshape(1)
    flips = sign_flips.reshape(local_rows // LANES, LANES)
    offsets = sample_offset.reshape(1, samples)
    y, z_low, z_high, core, x = (1 << bit for bit in range(dev_bits + grp_bits))
    scaling = 1.0 / math.sqrt(local_rows * count)
    across = (core, core)
    orders = [
        [(y, z_low), (z_low, y), (x, z_high), (z_high, x)],
        [(x, z_high), (z_high, x), (y, z_low), (z_low, y)],
    ]

    other = exchange(matrix_slab, core, across)
    other_flips = exchange(flips, core, across)
    other_offsets = exchange(offsets, core, across)
    own = call(
        functools.partial(own_kernel, scaling, core),
        block(columns // 2, local_rows),
        [IN_SMEM, IN_VMEM, IN_VMEM],
        [place, matrix_slab, flips],
    )
    chunk = block(2 * ROWS, local_rows)
    *chunks, tile = call(
        functools.partial(split_kernel, scaling, core),
        [chunk, chunk, block(ROWS, LANES)],
        [IN_SMEM] + [IN_VMEM] * 5,
        [place, own, other, other_flips, offsets, other_offsets],
    )
    almost, ridden, lasts = [], [], []
    for current, order in zip(chunks, orders):
        partner = exchange(current, core, order[0])
        current = call(
            functools.partial(mix_kernel, core, order[0]),
            block(2 * ROWS, local_rows + LANES),
            [IN_SMEM] + [IN_VMEM] * 3,
            [place, current, partner, tile],
        )
        partner = exchange(current, core, order[1])
        ridden.append(partner)
        current = call(
            functools.partial(second_kernel, core, order[1]),
            chunk,
            [IN_SMEM] + [IN_VMEM] * 2,
            [place, current, partner],
        )
        current = combine(current, exchange(current, core, order[2]), core, order[2])
        almost.append(current)
        lasts.append(
            call(
                functools.partial(last_kernel, core, order[3]),
                [block(ROWS, local_rows)] * 2,
                [IN_SMEM] + [IN_VMEM] * 2,
                [place, current, exchange(current, core, order[3])],
            )
        )
    last_masks = [order[3] for order in orders]
    shares = call(
        functools.partial(pick_kernel, core, last_masks),
        jax.ShapeDtypeStruct((count, samples // 2, LANES), jnp.float32),
        [IN_SMEM] + [IN_VMEM] * 5,
        [place, tile, *almost, *ridden[::-1]],
    )
    gram, sketch = call(
        functools.partial(gram_kernel, core, last_masks),
        [block(columns, columns), block(samples, columns)],
        [IN_SMEM, IN_VMEM],
        [place, lax.all_to_all(shares, AXES, 0, 0, tiled=True)],
    )
    kept = [keep for keep, _ in lasts]
    back = [exchange(send, core, across) for _, send in lasts]
    transformed = call(
        functools.partial(join_kernel, core),
        block(columns, local_rows),
        [IN_SMEM] + [IN_VMEM] * 4,
        [place, *kept, *back],
        out_specs=IN_HBM,
        scratch=[pltpu.SemaphoreType.DMA((4,))],
    )
    return (transformed, sketch.T, gram)


def solution(mesh):
    return jax.shard_map(
        local,
        mesh=mesh,
        in_specs=(P(None, AXES), P(AXES), P(AXES)),
        out_specs=(P(None, AXES), P(None, AXES), P()),
        check_vma=False,
    )
```

```python
import functools
import math

import jax
import jax.numpy as jnp
from jax import lax
from jax.experimental import pallas as pl
from jax.experimental.pallas import tpu as pltpu
from jax.sharding import PartitionSpec as P

AXES = ("grp", "dev")
LANES = 128
ROWS = 8
IN_VMEM = pl.BlockSpec(memory_space=pltpu.VMEM)
IN_SMEM = pl.BlockSpec(memory_space=pltpu.SMEM)
IN_HBM = pl.BlockSpec(memory_space=pltpu.HBM)


def call(body, outputs, in_specs, args, out_specs=None, scratch=()):
    return pl.pallas_call(
        body,
        out_shape=outputs,
        in_specs=in_specs,
        out_specs=jax.tree.map(lambda _: IN_VMEM, outputs) if out_specs is None else out_specs,
        scratch_shapes=scratch,
        compiler_params=pltpu.CompilerParams(vmem_limit_bytes=24 * 1024 * 1024),
    )(*args)


def block(rows, width, dtype=jnp.float32):
    return jax.ShapeDtypeStruct((rows, width), dtype)


def lanes_of(index):
    return slice(index * LANES, (index + 1) * LANES)


def exchange(array, core, masks):
    count = lax.axis_size(AXES)
    route = [(place, place ^ masks[0 if place & core == 0 else 1]) for place in range(count)]
    return lax.ppermute(array, AXES, route)


def chosen_mask(place, core, masks):
    return jnp.where(place & core == 0, masks[0], masks[1])


def three_parts(values):
    high = values.astype(jnp.bfloat16)
    rest = values - high.astype(jnp.float32)
    middle = rest.astype(jnp.bfloat16)
    low = (rest - middle.astype(jnp.float32)).astype(jnp.bfloat16)
    return high, middle, low


def exact_dot(values, table):
    total = None
    for piece in three_parts(values):
        product = jnp.dot(piece, table, preferred_element_type=jnp.float32)
        total = product if total is None else total + product
    return total


def mix(parts):
    left = lax.broadcasted_iota(jnp.int32, (LANES, LANES), 0)
    right = lax.broadcasted_iota(jnp.int32, (LANES, LANES), 1)
    parity = left & right
    for shift in (4, 2, 1):
        parity = parity ^ (parity >> shift)
    table = (1 - 2 * (parity & 1)).astype(jnp.float32).astype(jnp.bfloat16)
    parts = list(parts)
    span = 1
    while span < len(parts):
        for index in range(len(parts)):
            if index & span == 0:
                first, second = parts[index], parts[index | span]
                parts[index], parts[index | span] = first + second, first - second
        span *= 2
    total = exact_dot(jnp.concatenate(parts, axis=0), table)
    rows = parts[0].shape[0]
    return [total[index * rows : (index + 1) * rows] for index in range(len(parts))]


def own_kernel(scaling, core, place_ref, slab_ref, flips_ref, out_ref):
    columns = out_ref.shape[0]
    top = jnp.where(place_ref[0] & core == 0, 0, columns)
    for index in range(flips_ref.shape[0]):
        sign = jnp.where(flips_ref[index : index + 1, :] == 0, scaling, -scaling)
        rows = pl.ds(pl.multiple_of(top, ROWS), columns)
        out_ref[:, lanes_of(index)] = slab_ref[rows, lanes_of(index)] * sign


def split_kernel(scaling, core, place_ref, own_ref, other_ref, flips_ref, offset_ref, *out_refs):
    chunk_refs, spread_ref = out_refs[:-1], out_refs[-1]
    spread_ref[...] = jnp.concatenate([offset_ref[...]] * (LANES // offset_ref.shape[1]), axis=1)
    columns = own_ref.shape[0]
    on_first = place_ref[0] & core == 0
    top = jnp.where(on_first, 0, columns)
    turn = jnp.where(on_first, 1.0, -1.0)
    for index in range(flips_ref.shape[0]):
        here = lanes_of(index)
        sign = jnp.where(flips_ref[index : index + 1, :] == 0, scaling, -scaling)
        for number, chunk_ref in enumerate(chunk_refs):
            own = own_ref[number * ROWS : (number + 1) * ROWS, here]
            other = other_ref[pl.ds(pl.multiple_of(top + number * ROWS, ROWS), ROWS), here] * sign
            chunk_ref[:ROWS, here] = own + other
            chunk_ref[ROWS:, here] = (own - other) * turn


def tile_kernel(core, place_ref, offset_ref, other_offset_ref, tile_ref):
    samples = offset_ref.shape[1]
    own = jnp.concatenate([offset_ref[...]] * (LANES // samples), axis=1)
    lane = lax.broadcasted_iota(jnp.int32, (1, LANES), 1)
    own_first = jnp.where(place_ref[0] & core == 0, 0, 1)
    tile = jnp.where(lane // samples % 2 == own_first, own, other_offset_ref[...])
    tile_ref[...] = jnp.broadcast_to(tile.astype(jnp.float32), tile_ref.shape)


def mix_kernel(core, masks, place_ref, own_ref, other_ref, out_ref):
    slices = own_ref.shape[1] // LANES
    factor = jnp.where(place_ref[0] & chosen_mask(place_ref[0], core, masks) == 0, 1.0, -1.0)
    parts = [
        own_ref[:, lanes_of(index)] * factor + other_ref[:, lanes_of(index)] for index in range(slices)
    ]
    for index, part in enumerate(mix(parts)):
        out_ref[:, lanes_of(index)] = part


def ride_kernel(core, masks, place_ref, own_ref, other_ref, tile_ref, out_ref):
    width = own_ref.shape[1]
    factor = jnp.where(place_ref[0] & chosen_mask(place_ref[0], core, masks) == 0, 1.0, -1.0)
    out_ref[:, :width] = own_ref[...] * factor + other_ref[...]
    for row in range(0, own_ref.shape[0], ROWS):
        out_ref[row : row + ROWS, width:] = tile_ref[...]


def step_kernel(core, masks, place_ref, own_ref, other_ref, out_ref):
    factor = jnp.where(place_ref[0] & chosen_mask(place_ref[0], core, masks) == 0, 1.0, -1.0)
    width = out_ref.shape[1]
    out_ref[...] = own_ref[:, :width] * factor + other_ref[:, :width]


def pick(core, samples, masks, place_ref, tile_ref, chunk_ref, other_ref):
    lane = lax.broadcasted_iota(jnp.int32, (1, LANES), 1)
    place_in = lax.broadcasted_iota(jnp.int32, (LANES, LANES), 0)
    own_chip = lane < 2 * samples
    partner = other_ref[0:1, other_ref.shape[1] - LANES :]
    offsets = jnp.where(own_chip, tile_ref[0:1, :], partner).astype(jnp.int32)
    chosen = jnp.where(place_in == offsets % LANES, 1.0, 0.0).astype(jnp.bfloat16)
    side = jnp.where(place_ref[0] & chosen_mask(place_ref[0], core, masks) == 0, 1.0, -1.0)
    slices = chunk_ref.shape[1] // LANES
    rows = chunk_ref.shape[0]
    stacked = jnp.concatenate([chunk_ref[:, lanes_of(index)] for index in range(slices)], axis=0)
    found = exact_dot(stacked, chosen)
    share = jnp.zeros((rows, LANES), jnp.float32)
    for index in range(slices):
        share = jnp.where(offsets // LANES == index, found[index * rows : (index + 1) * rows], share)
    share = jnp.where(lane // samples % 2 == 0, share[:ROWS], share[ROWS:])
    return share * jnp.where(own_chip, side, 1.0)


def pick_kernel(core, samples, masks, place_ref, tile_ref, chunk_ref, other_ref, out_ref):
    out_ref[...] = pick(core, samples, masks, place_ref, tile_ref, chunk_ref, other_ref)


def pick_all_kernel(core, masks, place_ref, tile_ref, chunk_ref, other_ref, early_ref, out_ref):
    samples = out_ref.shape[1] * 2
    late = pick(core, samples, masks, place_ref, tile_ref, chunk_ref, other_ref)
    turned = jnp.concatenate([late, early_ref[...]], axis=0).T
    half = samples // 2
    starts = [
        (chip * 2 + second) * samples + part * half for part in range(2) for second in range(2) for chip in range(2)
    ]
    tile = jnp.concatenate([turned[start : start + half] for start in starts], axis=1)
    for place in range(out_ref.shape[0]):
        out_ref[place] = tile


def gram_kernel(core, all_masks, place_ref, shares_ref, after_ref, gram_ref, sketch_ref):
    count, rows, _ = shares_ref.shape
    columns = gram_ref.shape[0]
    width = columns // 2
    lane = lax.broadcasted_iota(jnp.int32, (rows, LANES), 1)
    number = lane % width // ROWS

    def of_core(place, second):
        others = shares_ref[place ^ all_masks[0][second]]
        for chunk in range(1, len(all_masks)):
            others = jnp.where(number == chunk, shares_ref[place ^ all_masks[chunk][second]], others)
        return shares_ref[place] + pltpu.roll(others, LANES - width, 1)

    def of_chip(place):
        second = pltpu.roll(of_core(place | core, 1), width, 1)
        return jnp.where(lane % columns < width, of_core(place, 0), second)

    chips = [place for place in range(count) if place & core == 0]
    stacked = jnp.concatenate([of_chip(place) for place in chips], axis=0)
    parts = [slice(start, start + columns) for start in range(0, LANES, columns)]
    products = lax.dot_general(
        stacked,
        stacked,
        (((0,), (0,)), ((), ())),
        precision=lax.Precision.HIGHEST,
        preferred_element_type=jnp.float32,
    )
    gram = sum([products[part, part] for part in parts[1:]], products[parts[0], parts[0]])
    gram_ref[...] = gram * (1.0 / (count * 2 * rows))
    own = of_chip(place_ref[0] & ~core)
    on_first = place_ref[0] & core == 0
    for half in range(2):
        first, second = own[:, parts[half * 2]], own[:, parts[half * 2 + 1]]
        sketch_ref[half * rows : (half + 1) * rows] = jnp.where(on_first, first, second)


def last_kernel(core, masks, place_ref, own_ref, other_ref, keep_ref, send_ref):
    on_first = place_ref[0] & core == 0
    factor = jnp.where(place_ref[0] & chosen_mask(place_ref[0], core, masks) == 0, 1.0, -1.0)
    for out_ref, top in ((keep_ref, jnp.where(on_first, 0, ROWS)), (send_ref, jnp.where(on_first, ROWS, 0))):
        rows = pl.ds(pl.multiple_of(top, ROWS), ROWS)
        out_ref[...] = own_ref[rows, :] * factor + other_ref[rows, :]


def join_kernel(core, place_ref, *refs):
    block_refs, (whole_ref, token_ref, sems) = refs[:-3], refs[-3:]
    token_ref[...] = jnp.zeros_like(token_ref)
    on_first = place_ref[0] & core == 0
    half = whole_ref.shape[0] // 2
    tops = []
    for kept in (True, False):
        base = jnp.where(on_first, 0, half) if kept else jnp.where(on_first, half, 0)
        tops += [base + row for row in range(0, half, ROWS)]
    copies = [
        pltpu.make_async_copy(
            block_ref, whole_ref.at[pl.ds(pl.multiple_of(top, ROWS), ROWS)], sems.at[number]
        )
        for number, (block_ref, top) in enumerate(zip(block_refs, tops))
    ]
    for copy in copies:
        copy.start()
    for copy in copies:
        copy.wait()


def local_any(matrix_slab, sign_flips, sample_offset):
    columns, local_rows = matrix_slab.shape
    count = lax.axis_size(AXES)
    samples = sample_offset.shape[0]
    numbers = jnp.arange(local_rows, dtype=jnp.int32)

    def table(order):
        common = numbers[:order, None] & numbers[None, :order]
        return (1 - 2 * (lax.population_count(common) & 1)).astype(jnp.float32)

    signs = (1 - 2 * sign_flips).astype(jnp.float32) * jnp.float32(1.0 / math.sqrt(local_rows * count))
    outer = local_rows // LANES
    shaped = (matrix_slab * signs[None, :]).reshape(columns, outer, LANES)
    shaped = jnp.einsum("cak,kz->caz", shaped, table(LANES), precision=lax.Precision.HIGHEST)
    shaped = jnp.einsum("cak,az->czk", shaped, table(outer), precision=lax.Precision.HIGHEST)
    current = shaped.reshape(columns, local_rows)
    for bit in range(count.bit_length() - 1):
        other = exchange(current, 1, (1 << bit, 1 << bit))
        lower = lax.axis_index(AXES) & 1 << bit == 0
        current = jnp.where(lower, current + other, other - current)
    sketch = jnp.take(current, sample_offset, axis=1)
    gram = jnp.dot(sketch, sketch.T, precision=lax.Precision.HIGHEST)
    return (current, sketch, lax.psum(gram, AXES) / jnp.float32(samples * count))


def local(matrix_slab, sign_flips, sample_offset):
    columns, local_rows = matrix_slab.shape
    grp_bits = lax.axis_size("grp").bit_length() - 1
    dev_bits = lax.axis_size("dev").bit_length() - 1
    count = lax.axis_size(AXES)
    samples = sample_offset.shape[0]
    if (grp_bits, dev_bits, columns, samples) != (2, 3, 4 * ROWS, 2 * ROWS):
        return local_any(matrix_slab, sign_flips, sample_offset)
    place = lax.axis_index(AXES).astype(jnp.int32).reshape(1)
    flips = sign_flips.reshape(local_rows // LANES, LANES)
    offsets = sample_offset.reshape(1, samples)
    y, z_low, z_high, core, x = (1 << bit for bit in range(dev_bits + grp_bits))
    scaling = 1.0 / math.sqrt(local_rows * count)
    across = (core, core)
    orders = [
        [(y, z_low), (x, z_high), (z_high, y), (z_low, x)],
        [(x, z_high), (y, z_low), (z_low, x), (z_high, y)],
    ]

    other = exchange(matrix_slab, core, across)
    other_flips = exchange(flips, core, across)
    other_offsets = exchange(offsets, core, across)
    own = call(
        functools.partial(own_kernel, scaling, core),
        block(columns // 2, local_rows),
        [IN_SMEM, IN_VMEM, IN_VMEM],
        [place, matrix_slab, flips],
    )
    chunk = block(2 * ROWS, local_rows)
    *chunks, spread = call(
        functools.partial(split_kernel, scaling, core),
        [chunk, chunk, block(1, LANES, jnp.int32)],
        [IN_SMEM] + [IN_VMEM] * 4,
        [place, own, other, other_flips, other_offsets],
    )
    tile = call(
        functools.partial(tile_kernel, core),
        block(ROWS, LANES),
        [IN_SMEM] + [IN_VMEM] * 2,
        [place, offsets, spread],
    )
    ridden, thirds = [], []
    for current, order in zip(chunks, orders):
        current = call(
            functools.partial(mix_kernel, core, order[0]),
            chunk,
            [IN_SMEM] + [IN_VMEM] * 2,
            [place, current, exchange(current, core, order[0])],
        )
        current = call(
            functools.partial(ride_kernel, core, order[1]),
            block(2 * ROWS, local_rows + LANES),
            [IN_SMEM] + [IN_VMEM] * 3,
            [place, current, exchange(current, core, order[1]), tile],
        )
        partner = exchange(current, core, order[2])
        ridden.append(partner)
        thirds.append(
            call(
                functools.partial(step_kernel, core, order[2]),
                chunk,
                [IN_SMEM] + [IN_VMEM] * 2,
                [place, current, partner],
            )
        )
    first, second = thirds
    last_masks = [order[3] for order in orders]
    early = call(
        functools.partial(pick_kernel, core, samples, last_masks[1]),
        block(ROWS, LANES),
        [IN_SMEM] + [IN_VMEM] * 3,
        [place, tile, second, ridden[0]],
    )
    shares = call(
        functools.partial(pick_all_kernel, core, last_masks[0]),
        jax.ShapeDtypeStruct((count, samples // 2, LANES), jnp.float32),
        [IN_SMEM] + [IN_VMEM] * 4,
        [place, tile, first, ridden[1], early],
    )
    lasts = [
        call(
            functools.partial(last_kernel, core, masks),
            [block(ROWS, local_rows)] * 2,
            [IN_SMEM] + [IN_VMEM] * 2,
            [place, current, exchange(current, core, masks)],
        )
        for current, masks in zip((first, second), last_masks)
    ]
    kept = [keep for keep, _ in lasts]
    back = [exchange(send, core, across) for _, send in lasts]
    transformed, token = call(
        functools.partial(join_kernel, core),
        [block(columns, local_rows), block(ROWS, LANES)],
        [IN_SMEM] + [IN_VMEM] * 4,
        [place, *kept, *back],
        out_specs=[IN_HBM, IN_VMEM],
        scratch=[pltpu.SemaphoreType.DMA((4,))],
    )
    gram, sketch = call(
        functools.partial(gram_kernel, core, last_masks),
        [block(columns, columns), block(samples, columns)],
        [IN_SMEM, IN_VMEM, IN_VMEM],
        [place, lax.all_to_all(shares, AXES, 0, 0, tiled=True), token],
    )
    return (transformed, sketch.T, gram)


def solution(mesh):
    return jax.shard_map(
        local,
        mesh=mesh,
        in_specs=(P(None, AXES), P(AXES), P(AXES)),
        out_specs=(P(None, AXES), P(None, AXES), P()),
        check_vma=False,
    )
```

```python
import functools
import math

import jax
import jax.numpy as jnp
from jax import lax
from jax.experimental import pallas as pl
from jax.experimental.pallas import tpu as pltpu
from jax.sharding import PartitionSpec as P

AXES = ("grp", "dev")
LANES = 128
ROWS = 8
IN_VMEM = pl.BlockSpec(memory_space=pltpu.VMEM)
IN_SMEM = pl.BlockSpec(memory_space=pltpu.SMEM)
IN_HBM = pl.BlockSpec(memory_space=pltpu.HBM)


def call(body, outputs, in_specs, args, out_specs=None, scratch=()):
    return pl.pallas_call(
        body,
        out_shape=outputs,
        in_specs=in_specs,
        out_specs=jax.tree.map(lambda _: IN_VMEM, outputs) if out_specs is None else out_specs,
        scratch_shapes=scratch,
        compiler_params=pltpu.CompilerParams(vmem_limit_bytes=24 * 1024 * 1024),
    )(*args)


def block(rows, width, dtype=jnp.float32):
    return jax.ShapeDtypeStruct((rows, width), dtype)


def lanes_of(index):
    return slice(index * LANES, (index + 1) * LANES)


def exchange(array, core, masks):
    count = lax.axis_size(AXES)
    route = [(place, place ^ masks[0 if place & core == 0 else 1]) for place in range(count)]
    return lax.ppermute(array, AXES, route)


def chosen_mask(place, core, masks):
    return jnp.where(place & core == 0, masks[0], masks[1])


def combine(current, partner, core, masks):
    place = lax.axis_index(AXES)
    lower = place & chosen_mask(place, core, masks) == 0
    return jnp.where(lower, current + partner, partner - current)


def three_parts(values):
    high = values.astype(jnp.bfloat16)
    rest = values - high.astype(jnp.float32)
    middle = rest.astype(jnp.bfloat16)
    low = (rest - middle.astype(jnp.float32)).astype(jnp.bfloat16)
    return high, middle, low


def exact_dot(values, table):
    total = None
    for piece in three_parts(values):
        product = jnp.dot(piece, table, preferred_element_type=jnp.float32)
        total = product if total is None else total + product
    return total


def mix(parts):
    left = lax.broadcasted_iota(jnp.int32, (LANES, LANES), 0)
    right = lax.broadcasted_iota(jnp.int32, (LANES, LANES), 1)
    parity = left & right
    for shift in (4, 2, 1):
        parity = parity ^ (parity >> shift)
    table = (1 - 2 * (parity & 1)).astype(jnp.float32).astype(jnp.bfloat16)
    parts = list(parts)
    span = 1
    while span < len(parts):
        for index in range(len(parts)):
            if index & span == 0:
                first, second = parts[index], parts[index | span]
                parts[index], parts[index | span] = first + second, first - second
        span *= 2
    total = exact_dot(jnp.concatenate(parts, axis=0), table)
    rows = parts[0].shape[0]
    return [total[index * rows : (index + 1) * rows] for index in range(len(parts))]


def own_kernel(scaling, core, place_ref, slab_ref, flips_ref, out_ref):
    columns = out_ref.shape[0]
    top = jnp.where(place_ref[0] & core == 0, 0, columns)
    for index in range(flips_ref.shape[0]):
        sign = jnp.where(flips_ref[index : index + 1, :] == 0, scaling, -scaling)
        rows = pl.ds(pl.multiple_of(top, ROWS), columns)
        out_ref[:, lanes_of(index)] = slab_ref[rows, lanes_of(index)] * sign


def split_kernel(scaling, core, place_ref, own_ref, other_ref, flips_ref, offset_ref, *out_refs):
    chunk_refs, spread_ref = out_refs[:-1], out_refs[-1]
    spread_ref[...] = jnp.concatenate([offset_ref[...]] * (LANES // offset_ref.shape[1]), axis=1)
    columns = own_ref.shape[0]
    on_first = place_ref[0] & core == 0
    top = jnp.where(on_first, 0, columns)
    turn = jnp.where(on_first, 1.0, -1.0)
    for index in range(flips_ref.shape[0]):
        here = lanes_of(index)
        sign = jnp.where(flips_ref[index : index + 1, :] == 0, scaling, -scaling)
        for number, chunk_ref in enumerate(chunk_refs):
            own = own_ref[number * ROWS : (number + 1) * ROWS, here]
            other = other_ref[pl.ds(pl.multiple_of(top + number * ROWS, ROWS), ROWS), here] * sign
            chunk_ref[:ROWS, here] = own + other
            chunk_ref[ROWS:, here] = (own - other) * turn


def tile_kernel(core, place_ref, offset_ref, other_offset_ref, tile_ref):
    samples = offset_ref.shape[1]
    own = jnp.concatenate([offset_ref[...]] * (LANES // samples), axis=1)
    lane = lax.broadcasted_iota(jnp.int32, (1, LANES), 1)
    own_first = jnp.where(place_ref[0] & core == 0, 0, 1)
    tile = jnp.where(lane // samples % 2 == own_first, own, other_offset_ref[...])
    tile_ref[...] = jnp.broadcast_to(tile.astype(jnp.float32), tile_ref.shape)


def mix_kernel(core, masks, place_ref, own_ref, other_ref, tile_ref, out_ref):
    slices = own_ref.shape[1] // LANES
    factor = jnp.where(place_ref[0] & chosen_mask(place_ref[0], core, masks) == 0, 1.0, -1.0)
    parts = [
        own_ref[:, lanes_of(index)] * factor + other_ref[:, lanes_of(index)] for index in range(slices)
    ]
    for index, part in enumerate(mix(parts)):
        out_ref[:, lanes_of(index)] = part
    for row in range(0, own_ref.shape[0], ROWS):
        out_ref[row : row + ROWS, lanes_of(slices)] = tile_ref[...]


def step_kernel(core, masks, place_ref, own_ref, other_ref, out_ref):
    factor = jnp.where(place_ref[0] & chosen_mask(place_ref[0], core, masks) == 0, 1.0, -1.0)
    width = out_ref.shape[1]
    out_ref[...] = own_ref[:, :width] * factor + other_ref[:, :width]


def step_after_kernel(core, masks, place_ref, own_ref, other_ref, after_ref, out_ref):
    step_kernel(core, masks, place_ref, own_ref, other_ref, out_ref)


def pick(core, samples, masks, place_ref, tile_ref, chunk_ref, other_ref):
    lane = lax.broadcasted_iota(jnp.int32, (1, LANES), 1)
    place_in = lax.broadcasted_iota(jnp.int32, (LANES, LANES), 0)
    own_chip = lane < 2 * samples
    partner = other_ref[0:1, other_ref.shape[1] - LANES :]
    offsets = jnp.where(own_chip, tile_ref[0:1, :], partner).astype(jnp.int32)
    chosen = jnp.where(place_in == offsets % LANES, 1.0, 0.0).astype(jnp.bfloat16)
    side = jnp.where(place_ref[0] & chosen_mask(place_ref[0], core, masks) == 0, 1.0, -1.0)
    slices = chunk_ref.shape[1] // LANES
    rows = chunk_ref.shape[0]
    stacked = jnp.concatenate([chunk_ref[:, lanes_of(index)] for index in range(slices)], axis=0)
    found = exact_dot(stacked, chosen)
    share = jnp.zeros((rows, LANES), jnp.float32)
    for index in range(slices):
        share = jnp.where(offsets // LANES == index, found[index * rows : (index + 1) * rows], share)
    share = jnp.where(lane // samples % 2 == 0, share[:ROWS], share[ROWS:])
    return share * jnp.where(own_chip, side, 1.0)


def pick_kernel(core, samples, masks, place_ref, tile_ref, chunk_ref, other_ref, out_ref):
    out_ref[...] = pick(core, samples, masks, place_ref, tile_ref, chunk_ref, other_ref)


def pick_all_kernel(core, samples, masks, place_ref, tile_ref, chunk_ref, other_ref, early_ref, out_ref):
    late = pick(core, samples, masks, place_ref, tile_ref, chunk_ref, other_ref)
    lane = lax.broadcasted_iota(jnp.int32, late.shape, 1)
    tile = jnp.where(lane < LANES // 2, late, pltpu.roll(early_ref[...], LANES // 2, 1))
    for place in range(out_ref.shape[0]):
        out_ref[place] = tile


def gram_kernel(core, all_masks, place_ref, shares_ref, after_ref, gram_ref, sketch_ref):
    count, rows, _ = shares_ref.shape
    samples = sketch_ref.shape[0]
    width, half = 2 * samples, LANES // 2
    lane = lax.broadcasted_iota(jnp.int32, (rows, LANES), 1)

    def of_core(place, second):
        first, last = (shares_ref[place ^ masks[second]] for masks in all_masks)
        return shares_ref[place] + pltpu.roll(jnp.where(lane < half, first, last), LANES - width, 1)

    def moved(values, start):
        return pltpu.roll(values, start, 1) if start % LANES else values

    chips = [place for place in range(count) if place & core == 0]
    wraps = []
    for wrap in range(0, len(chips), LANES // width):
        rows_of_all = []
        for second in range(2):
            parts = [of_core(chip | core * second, second) for chip in chips[wrap : wrap + LANES // width]]
            for chunk in range(2):
                joined = moved(parts[0], chunk * half)
                for number in range(1, len(parts)):
                    here = moved(parts[number], (number * width + chunk * half) % LANES)
                    joined = jnp.where(lane >= number * width, here, joined)
                rows_of_all.append(joined)
        wraps.append(jnp.concatenate(rows_of_all, axis=0))
    sketch = jnp.concatenate(wraps, axis=1)
    product = functools.partial(
        lax.dot_general,
        dimension_numbers=(((1,), (1,)), ((), ())),
        precision=lax.Precision.HIGHEST,
        preferred_element_type=jnp.float32,
    )
    gram_ref[...] = product(sketch, sketch) * (1.0 / (count * samples))
    chip = place_ref[0] & ~core
    own = []
    for second in range(2):
        part = of_core(chip | core * second, second)
        own += [part, moved(part, half)]
    start = jnp.where(place_ref[0] & core == 0, 0, samples)
    row = lax.broadcasted_iota(jnp.int32, (samples, LANES), 0)
    spot = lax.broadcasted_iota(jnp.int32, (samples, LANES), 1)
    sketch_ref[...] = product(jnp.where(spot == row + start, 1.0, 0.0), jnp.concatenate(own, axis=0))


def last_kernel(core, masks, place_ref, own_ref, other_ref, keep_ref, send_ref):
    on_first = place_ref[0] & core == 0
    factor = jnp.where(place_ref[0] & chosen_mask(place_ref[0], core, masks) == 0, 1.0, -1.0)
    for out_ref, top in ((keep_ref, jnp.where(on_first, 0, ROWS)), (send_ref, jnp.where(on_first, ROWS, 0))):
        rows = pl.ds(pl.multiple_of(top, ROWS), ROWS)
        out_ref[...] = own_ref[rows, :] * factor + other_ref[rows, :]


def join_kernel(core, place_ref, *refs):
    block_refs, (whole_ref, token_ref, sems) = refs[:-3], refs[-3:]
    token_ref[...] = jnp.zeros_like(token_ref)
    on_first = place_ref[0] & core == 0
    half = whole_ref.shape[0] // 2
    tops = []
    for kept in (True, False):
        base = jnp.where(on_first, 0, half) if kept else jnp.where(on_first, half, 0)
        tops += [base + row for row in range(0, half, ROWS)]
    copies = [
        pltpu.make_async_copy(
            block_ref, whole_ref.at[pl.ds(pl.multiple_of(top, ROWS), ROWS)], sems.at[number]
        )
        for number, (block_ref, top) in enumerate(zip(block_refs, tops))
    ]
    for copy in copies:
        copy.start()
    for copy in copies:
        copy.wait()


def local_any(matrix_slab, sign_flips, sample_offset):
    columns, local_rows = matrix_slab.shape
    count = lax.axis_size(AXES)
    samples = sample_offset.shape[0]
    numbers = jnp.arange(local_rows, dtype=jnp.int32)

    def table(order):
        common = numbers[:order, None] & numbers[None, :order]
        return (1 - 2 * (lax.population_count(common) & 1)).astype(jnp.float32)

    signs = (1 - 2 * sign_flips).astype(jnp.float32) * jnp.float32(1.0 / math.sqrt(local_rows * count))
    outer = local_rows // LANES
    shaped = (matrix_slab * signs[None, :]).reshape(columns, outer, LANES)
    shaped = jnp.einsum("cak,kz->caz", shaped, table(LANES), precision=lax.Precision.HIGHEST)
    shaped = jnp.einsum("cak,az->czk", shaped, table(outer), precision=lax.Precision.HIGHEST)
    current = shaped.reshape(columns, local_rows)
    for bit in range(count.bit_length() - 1):
        masks = (1 << bit, 1 << bit)
        current = combine(current, exchange(current, 1, masks), 1, masks)
    sketch = jnp.take(current, sample_offset, axis=1)
    gram = jnp.dot(sketch, sketch.T, precision=lax.Precision.HIGHEST)
    return (current, sketch, lax.psum(gram, AXES) / jnp.float32(samples * count))


def local(matrix_slab, sign_flips, sample_offset):
    columns, local_rows = matrix_slab.shape
    grp_bits = lax.axis_size("grp").bit_length() - 1
    dev_bits = lax.axis_size("dev").bit_length() - 1
    count = lax.axis_size(AXES)
    samples = sample_offset.shape[0]
    if (grp_bits, dev_bits, columns, samples) != (2, 3, 4 * ROWS, 2 * ROWS):
        return local_any(matrix_slab, sign_flips, sample_offset)
    place = lax.axis_index(AXES).astype(jnp.int32).reshape(1)
    flips = sign_flips.reshape(local_rows // LANES, LANES)
    offsets = sample_offset.reshape(1, samples)
    y, z_low, z_high, core, x = (1 << bit for bit in range(dev_bits + grp_bits))
    scaling = 1.0 / math.sqrt(local_rows * count)
    across = (core, core)
    orders = [
        [(y, z_low), (z_low, y), (x, z_high), (z_high, x)],
        [(x, z_high), (z_high, x), (y, z_low), (z_low, y)],
    ]

    other = exchange(matrix_slab, core, across)
    other_flips = exchange(flips, core, across)
    other_offsets = exchange(offsets, core, across)
    own = call(
        functools.partial(own_kernel, scaling, core),
        block(columns // 2, local_rows),
        [IN_SMEM, IN_VMEM, IN_VMEM],
        [place, matrix_slab, flips],
    )
    chunk = block(2 * ROWS, local_rows)
    *chunks, spread = call(
        functools.partial(split_kernel, scaling, core),
        [chunk, chunk, block(1, LANES, jnp.int32)],
        [IN_SMEM] + [IN_VMEM] * 4,
        [place, own, other, other_flips, other_offsets],
    )
    tile = call(
        functools.partial(tile_kernel, core),
        block(ROWS, LANES),
        [IN_SMEM] + [IN_VMEM] * 2,
        [place, offsets, spread],
    )
    ridden, thirds = [], []
    for current, order in zip(chunks, orders):
        partner = exchange(current, core, order[0])
        current = call(
            functools.partial(mix_kernel, core, order[0]),
            block(2 * ROWS, local_rows + LANES),
            [IN_SMEM] + [IN_VMEM] * 3,
            [place, current, partner, tile],
        )
        partner = exchange(current, core, order[1])
        ridden.append(partner)
        current = call(
            functools.partial(step_kernel, core, order[1]),
            chunk,
            [IN_SMEM] + [IN_VMEM] * 2,
            [place, current, partner],
        )
        thirds.append((current, exchange(current, core, order[2])))
    last_masks = [order[3] for order in orders]
    second = combine(*thirds[1], core, orders[1][2])
    early = call(
        functools.partial(pick_kernel, core, samples, last_masks[1]),
        block(ROWS, LANES),
        [IN_SMEM] + [IN_VMEM] * 3,
        [place, tile, second, ridden[0]],
    )
    first = call(
        functools.partial(step_after_kernel, core, orders[0][2]),
        chunk,
        [IN_SMEM] + [IN_VMEM] * 3,
        [place, *thirds[0], early],
    )
    shares = call(
        functools.partial(pick_all_kernel, core, samples, last_masks[0]),
        jax.ShapeDtypeStruct((count, ROWS, LANES), jnp.float32),
        [IN_SMEM] + [IN_VMEM] * 4,
        [place, tile, first, ridden[1], early],
    )
    lasts = [
        call(
            functools.partial(last_kernel, core, masks),
            [block(ROWS, local_rows)] * 2,
            [IN_SMEM] + [IN_VMEM] * 2,
            [place, current, exchange(current, core, masks)],
        )
        for current, masks in zip((first, second), last_masks)
    ]
    kept = [keep for keep, _ in lasts]
    back = [exchange(send, core, across) for _, send in lasts]
    transformed, token = call(
        functools.partial(join_kernel, core),
        [block(columns, local_rows), block(ROWS, LANES)],
        [IN_SMEM] + [IN_VMEM] * 4,
        [place, *kept, *back],
        out_specs=[IN_HBM, IN_VMEM],
        scratch=[pltpu.SemaphoreType.DMA((4,))],
    )
    gram, sketch = call(
        functools.partial(gram_kernel, core, last_masks),
        [block(columns, columns), block(samples, columns)],
        [IN_SMEM, IN_VMEM, IN_VMEM],
        [place, lax.all_to_all(shares, AXES, 0, 0, tiled=True), token],
    )
    return (transformed, sketch.T, gram)


def solution(mesh):
    return jax.shard_map(
        local,
        mesh=mesh,
        in_specs=(P(None, AXES), P(AXES), P(AXES)),
        out_specs=(P(None, AXES), P(None, AXES), P()),
        check_vma=False,
    )
```

```python
import functools
import math

import jax
import jax.numpy as jnp
from jax import lax
from jax.experimental import pallas as pl
from jax.experimental.pallas import tpu as pltpu
from jax.sharding import PartitionSpec as P

AXES = ("grp", "dev")
LANES = 128
ROWS = 8
IN_VMEM = pl.BlockSpec(memory_space=pltpu.VMEM)
IN_SMEM = pl.BlockSpec(memory_space=pltpu.SMEM)
IN_HBM = pl.BlockSpec(memory_space=pltpu.HBM)


def call(body, outputs, in_specs, args, out_specs=None, scratch=()):
    return pl.pallas_call(
        body,
        out_shape=outputs,
        in_specs=in_specs,
        out_specs=jax.tree.map(lambda _: IN_VMEM, outputs) if out_specs is None else out_specs,
        scratch_shapes=scratch,
        compiler_params=pltpu.CompilerParams(vmem_limit_bytes=24 * 1024 * 1024),
    )(*args)


def block(rows, width, dtype=jnp.float32):
    return jax.ShapeDtypeStruct((rows, width), dtype)


def lanes_of(index):
    return slice(index * LANES, (index + 1) * LANES)


def exchange(array, core, masks):
    count = lax.axis_size(AXES)
    route = [(place, place ^ masks[0 if place & core == 0 else 1]) for place in range(count)]
    return lax.ppermute(array, AXES, route)


def chosen_mask(place, core, masks):
    return jnp.where(place & core == 0, masks[0], masks[1])


def combine(current, partner, core, masks):
    place = lax.axis_index(AXES)
    lower = place & chosen_mask(place, core, masks) == 0
    return jnp.where(lower, current + partner, partner - current)


def three_parts(values):
    high = values.astype(jnp.bfloat16)
    rest = values - high.astype(jnp.float32)
    middle = rest.astype(jnp.bfloat16)
    low = (rest - middle.astype(jnp.float32)).astype(jnp.bfloat16)
    return high, middle, low


def exact_dot(values, table):
    total = None
    for piece in three_parts(values):
        product = jnp.dot(piece, table, preferred_element_type=jnp.float32)
        total = product if total is None else total + product
    return total


def sign_of(left, right):
    parity = left & right
    for shift in (4, 2, 1):
        parity = parity ^ (parity >> shift)
    return (1 - 2 * (parity & 1)).astype(jnp.float32)


def mix(parts):
    left = lax.broadcasted_iota(jnp.int32, (LANES, LANES), 0)
    right = lax.broadcasted_iota(jnp.int32, (LANES, LANES), 1)
    table = sign_of(left, right).astype(jnp.bfloat16)
    parts = list(parts)
    span = 1
    while span < len(parts):
        for index in range(len(parts)):
            if index & span == 0:
                first, second = parts[index], parts[index | span]
                parts[index], parts[index | span] = first + second, first - second
        span *= 2
    total = exact_dot(jnp.concatenate(parts, axis=0), table)
    rows = parts[0].shape[0]
    return [total[index * rows : (index + 1) * rows] for index in range(len(parts))]


def own_kernel(scaling, core, place_ref, slab_ref, flips_ref, out_ref):
    columns = out_ref.shape[0]
    top = jnp.where(place_ref[0] & core == 0, 0, columns)
    for index in range(flips_ref.shape[0]):
        sign = jnp.where(flips_ref[index : index + 1, :] == 0, scaling, -scaling)
        rows = pl.ds(pl.multiple_of(top, ROWS), columns)
        out_ref[:, lanes_of(index)] = slab_ref[rows, lanes_of(index)] * sign


def split_kernel(scaling, core, place_ref, own_ref, other_ref, flips_ref, offset_ref, *out_refs):
    chunk_refs, spread_ref = out_refs[:-1], out_refs[-1]
    spread_ref[...] = jnp.concatenate([offset_ref[...]] * (LANES // offset_ref.shape[1]), axis=1)
    columns = own_ref.shape[0]
    on_first = place_ref[0] & core == 0
    top = jnp.where(on_first, 0, columns)
    turn = jnp.where(on_first, 1.0, -1.0)
    for index in range(flips_ref.shape[0]):
        here = lanes_of(index)
        sign = jnp.where(flips_ref[index : index + 1, :] == 0, scaling, -scaling)
        for number, chunk_ref in enumerate(chunk_refs):
            own = own_ref[number * ROWS : (number + 1) * ROWS, here]
            other = other_ref[pl.ds(pl.multiple_of(top + number * ROWS, ROWS), ROWS), here] * sign
            chunk_ref[:ROWS, here] = own + other
            chunk_ref[ROWS:, here] = (own - other) * turn


def tile_kernel(core, place_ref, offset_ref, other_offset_ref, tile_ref):
    samples = offset_ref.shape[1]
    own = jnp.concatenate([offset_ref[...]] * (LANES // samples), axis=1)
    lane = lax.broadcasted_iota(jnp.int32, (1, LANES), 1)
    own_first = jnp.where(place_ref[0] & core == 0, 0, 1)
    tile = jnp.where(lane // samples % 2 == own_first, own, other_offset_ref[...])
    tile_ref[...] = jnp.broadcast_to(tile.astype(jnp.float32), tile_ref.shape)


def ride_kernel(core, masks, place_ref, own_ref, other_ref, tile_ref, out_ref):
    width = own_ref.shape[1]
    factor = jnp.where(place_ref[0] & chosen_mask(place_ref[0], core, masks) == 0, 1.0, -1.0)
    out_ref[:, :width] = own_ref[...] * factor + other_ref[...]
    for row in range(0, own_ref.shape[0], ROWS):
        out_ref[row : row + ROWS, width:] = tile_ref[...]


def step_kernel(core, masks, place_ref, own_ref, other_ref, out_ref):
    factor = jnp.where(place_ref[0] & chosen_mask(place_ref[0], core, masks) == 0, 1.0, -1.0)
    width = out_ref.shape[1]
    out_ref[...] = own_ref[:, :width] * factor + other_ref[:, :width]


def step_after_kernel(core, masks, place_ref, own_ref, other_ref, after_ref, out_ref):
    step_kernel(core, masks, place_ref, own_ref, other_ref, out_ref)


def pick(core, samples, masks, place_ref, tile_ref, chunk_ref, other_ref):
    lane = lax.broadcasted_iota(jnp.int32, (1, LANES), 1)
    place_in = lax.broadcasted_iota(jnp.int32, (LANES, LANES), 0)
    own_chip = lane < 2 * samples
    partner = other_ref[0:1, other_ref.shape[1] - LANES :]
    offsets = jnp.where(own_chip, tile_ref[0:1, :], partner).astype(jnp.int32)
    signs = sign_of(place_in, offsets % LANES).astype(jnp.bfloat16)
    side = jnp.where(place_ref[0] & chosen_mask(place_ref[0], core, masks) == 0, 1.0, -1.0)
    slices = chunk_ref.shape[1] // LANES
    rows = chunk_ref.shape[0]
    stacked = jnp.concatenate([chunk_ref[:, lanes_of(index)] for index in range(slices)], axis=0)
    found = exact_dot(stacked, signs)
    share = found[:rows]
    for index in range(1, slices):
        share = share + found[index * rows : (index + 1) * rows] * sign_of(offsets // LANES, index)
    share = jnp.where(lane // samples % 2 == 0, share[:ROWS], share[ROWS:])
    return share * jnp.where(own_chip, side, 1.0)


def pick_kernel(core, samples, masks, place_ref, tile_ref, chunk_ref, other_ref, out_ref):
    out_ref[...] = pick(core, samples, masks, place_ref, tile_ref, chunk_ref, other_ref)


def pick_all_kernel(core, samples, masks, place_ref, tile_ref, chunk_ref, other_ref, early_ref, out_ref, token_ref):
    token_ref[...] = jnp.zeros_like(token_ref)
    late = pick(core, samples, masks, place_ref, tile_ref, chunk_ref, other_ref)
    lane = lax.broadcasted_iota(jnp.int32, late.shape, 1)
    tile = jnp.where(lane < LANES // 2, late, pltpu.roll(early_ref[...], LANES // 2, 1))
    for place in range(out_ref.shape[0]):
        out_ref[place] = tile


def gram_kernel(core, all_masks, place_ref, shares_ref, after_ref, gram_ref, sketch_ref):
    count, rows, _ = shares_ref.shape
    samples = sketch_ref.shape[0]
    width, half = 2 * samples, LANES // 2
    lane = lax.broadcasted_iota(jnp.int32, (rows, LANES), 1)

    def of_core(place, second):
        first, last = (shares_ref[place ^ masks[second]] for masks in all_masks)
        return shares_ref[place] + pltpu.roll(jnp.where(lane < half, first, last), LANES - width, 1)

    def moved(values, start):
        return pltpu.roll(values, start, 1) if start % LANES else values

    chips = [place for place in range(count) if place & core == 0]
    wraps = []
    for wrap in range(0, len(chips), LANES // width):
        rows_of_all = []
        for second in range(2):
            parts = [of_core(chip | core * second, second) for chip in chips[wrap : wrap + LANES // width]]
            for chunk in range(2):
                joined = moved(parts[0], chunk * half)
                for number in range(1, len(parts)):
                    here = moved(parts[number], (number * width + chunk * half) % LANES)
                    joined = jnp.where(lane >= number * width, here, joined)
                rows_of_all.append(joined)
        wraps.append(jnp.concatenate(rows_of_all, axis=0))
    sketch = jnp.concatenate(wraps, axis=1)
    product = functools.partial(
        lax.dot_general,
        dimension_numbers=(((1,), (1,)), ((), ())),
        precision=lax.Precision.HIGHEST,
        preferred_element_type=jnp.float32,
    )
    gram_ref[...] = product(sketch, sketch) * (1.0 / (count * samples))
    chip = place_ref[0] & ~core
    own = []
    for second in range(2):
        part = of_core(chip | core * second, second)
        own += [part, moved(part, half)]
    start = jnp.where(place_ref[0] & core == 0, 0, samples)
    row = lax.broadcasted_iota(jnp.int32, (samples, LANES), 0)
    spot = lax.broadcasted_iota(jnp.int32, (samples, LANES), 1)
    sketch_ref[...] = product(jnp.where(spot == row + start, 1.0, 0.0), jnp.concatenate(own, axis=0))


def last_kernel(core, masks, place_ref, own_ref, other_ref, after_ref, keep_ref, send_ref):
    on_first = place_ref[0] & core == 0
    factor = jnp.where(place_ref[0] & chosen_mask(place_ref[0], core, masks) == 0, 1.0, -1.0)
    for out_ref, top in ((keep_ref, jnp.where(on_first, 0, ROWS)), (send_ref, jnp.where(on_first, ROWS, 0))):
        rows = pl.ds(pl.multiple_of(top, ROWS), ROWS)
        slices = out_ref.shape[1] // LANES
        parts = [
            own_ref[rows, lanes_of(index)] * factor + other_ref[rows, lanes_of(index)] for index in range(slices)
        ]
        for index, part in enumerate(mix(parts)):
            out_ref[:, lanes_of(index)] = part


def join_kernel(core, place_ref, *refs):
    block_refs, (whole_ref, token_ref, sems) = refs[:-3], refs[-3:]
    token_ref[...] = jnp.zeros_like(token_ref)
    on_first = place_ref[0] & core == 0
    half = whole_ref.shape[0] // 2
    tops = []
    for kept in (True, False):
        base = jnp.where(on_first, 0, half) if kept else jnp.where(on_first, half, 0)
        tops += [base + row for row in range(0, half, ROWS)]
    copies = [
        pltpu.make_async_copy(
            block_ref, whole_ref.at[pl.ds(pl.multiple_of(top, ROWS), ROWS)], sems.at[number]
        )
        for number, (block_ref, top) in enumerate(zip(block_refs, tops))
    ]
    for copy in copies:
        copy.start()
    for copy in copies:
        copy.wait()


def local_any(matrix_slab, sign_flips, sample_offset):
    columns, local_rows = matrix_slab.shape
    count = lax.axis_size(AXES)
    samples = sample_offset.shape[0]
    numbers = jnp.arange(local_rows, dtype=jnp.int32)

    def table(order):
        common = numbers[:order, None] & numbers[None, :order]
        return (1 - 2 * (lax.population_count(common) & 1)).astype(jnp.float32)

    signs = (1 - 2 * sign_flips).astype(jnp.float32) * jnp.float32(1.0 / math.sqrt(local_rows * count))
    outer = local_rows // LANES
    shaped = (matrix_slab * signs[None, :]).reshape(columns, outer, LANES)
    shaped = jnp.einsum("cak,kz->caz", shaped, table(LANES), precision=lax.Precision.HIGHEST)
    shaped = jnp.einsum("cak,az->czk", shaped, table(outer), precision=lax.Precision.HIGHEST)
    current = shaped.reshape(columns, local_rows)
    for bit in range(count.bit_length() - 1):
        masks = (1 << bit, 1 << bit)
        current = combine(current, exchange(current, 1, masks), 1, masks)
    sketch = jnp.take(current, sample_offset, axis=1)
    gram = jnp.dot(sketch, sketch.T, precision=lax.Precision.HIGHEST)
    return (current, sketch, lax.psum(gram, AXES) / jnp.float32(samples * count))


def local(matrix_slab, sign_flips, sample_offset):
    columns, local_rows = matrix_slab.shape
    grp_bits = lax.axis_size("grp").bit_length() - 1
    dev_bits = lax.axis_size("dev").bit_length() - 1
    count = lax.axis_size(AXES)
    samples = sample_offset.shape[0]
    if (grp_bits, dev_bits, columns, samples) != (2, 3, 4 * ROWS, 2 * ROWS):
        return local_any(matrix_slab, sign_flips, sample_offset)
    place = lax.axis_index(AXES).astype(jnp.int32).reshape(1)
    flips = sign_flips.reshape(local_rows // LANES, LANES)
    offsets = sample_offset.reshape(1, samples)
    y, z_low, z_high, core, x = (1 << bit for bit in range(dev_bits + grp_bits))
    scaling = 1.0 / math.sqrt(local_rows * count)
    across = (core, core)
    orders = [
        [(y, z_low), (z_low, y), (x, z_high), (z_high, x)],
        [(x, z_high), (z_high, x), (y, z_low), (z_low, y)],
    ]

    other = exchange(matrix_slab, core, across)
    other_flips = exchange(flips, core, across)
    other_offsets = exchange(offsets, core, across)
    own = call(
        functools.partial(own_kernel, scaling, core),
        block(columns // 2, local_rows),
        [IN_SMEM, IN_VMEM, IN_VMEM],
        [place, matrix_slab, flips],
    )
    chunk = block(2 * ROWS, local_rows)
    *chunks, spread = call(
        functools.partial(split_kernel, scaling, core),
        [chunk, chunk, block(1, LANES, jnp.int32)],
        [IN_SMEM] + [IN_VMEM] * 4,
        [place, own, other, other_flips, other_offsets],
    )
    tile = call(
        functools.partial(tile_kernel, core),
        block(ROWS, LANES),
        [IN_SMEM] + [IN_VMEM] * 2,
        [place, offsets, spread],
    )
    ridden, thirds = [], []
    for current, order in zip(chunks, orders):
        partner = exchange(current, core, order[0])
        current = call(
            functools.partial(ride_kernel, core, order[0]),
            block(2 * ROWS, local_rows + LANES),
            [IN_SMEM] + [IN_VMEM] * 3,
            [place, current, partner, tile],
        )
        partner = exchange(current, core, order[1])
        ridden.append(partner)
        current = call(
            functools.partial(step_kernel, core, order[1]),
            chunk,
            [IN_SMEM] + [IN_VMEM] * 2,
            [place, current, partner],
        )
        thirds.append((current, exchange(current, core, order[2])))
    last_masks = [order[3] for order in orders]
    second = combine(*thirds[1], core, orders[1][2])
    early = call(
        functools.partial(pick_kernel, core, samples, last_masks[1]),
        block(ROWS, LANES),
        [IN_SMEM] + [IN_VMEM] * 3,
        [place, tile, second, ridden[0]],
    )
    first = call(
        functools.partial(step_after_kernel, core, orders[0][2]),
        chunk,
        [IN_SMEM] + [IN_VMEM] * 3,
        [place, *thirds[0], early],
    )
    shares, picked = call(
        functools.partial(pick_all_kernel, core, samples, last_masks[0]),
        [jax.ShapeDtypeStruct((count, ROWS, LANES), jnp.float32), block(ROWS, LANES)],
        [IN_SMEM] + [IN_VMEM] * 4,
        [place, tile, first, ridden[1], early],
    )
    later = call(
        functools.partial(step_after_kernel, core, orders[1][2]),
        chunk,
        [IN_SMEM] + [IN_VMEM] * 3,
        [place, *thirds[1], picked],
    )
    lasts = [
        call(
            functools.partial(last_kernel, core, last_masks[0]),
            [block(ROWS, local_rows)] * 2,
            [IN_SMEM] + [IN_VMEM] * 3,
            [place, first, exchange(first, core, last_masks[0]), picked],
        )
    ]
    lasts.append(
        call(
            functools.partial(last_kernel, core, last_masks[1]),
            [block(ROWS, local_rows)] * 2,
            [IN_SMEM] + [IN_VMEM] * 3,
            [place, later, exchange(later, core, last_masks[1]), lasts[0][0]],
        )
    )
    kept = [keep for keep, _ in lasts]
    back = [exchange(send, core, across) for _, send in lasts]
    transformed, token = call(
        functools.partial(join_kernel, core),
        [block(columns, local_rows), block(ROWS, LANES)],
        [IN_SMEM] + [IN_VMEM] * 4,
        [place, *kept, *back],
        out_specs=[IN_HBM, IN_VMEM],
        scratch=[pltpu.SemaphoreType.DMA((4,))],
    )
    gram, sketch = call(
        functools.partial(gram_kernel, core, last_masks),
        [block(columns, columns), block(samples, columns)],
        [IN_SMEM, IN_VMEM, IN_VMEM],
        [place, lax.all_to_all(shares, AXES, 0, 0, tiled=True), token],
    )
    return (transformed, sketch.T, gram)


def solution(mesh):
    return jax.shard_map(
        local,
        mesh=mesh,
        in_specs=(P(None, AXES), P(AXES), P(AXES)),
        out_specs=(P(None, AXES), P(None, AXES), P()),
        check_vma=False,
    )
```

```python
import functools
import math

import jax
import jax.numpy as jnp
from jax import lax
from jax.experimental import pallas as pl
from jax.experimental.pallas import tpu as pltpu
from jax.sharding import PartitionSpec as P

AXES = ("grp", "dev")
LANES = 128
ROWS = 8
IN_VMEM = pl.BlockSpec(memory_space=pltpu.VMEM)
IN_SMEM = pl.BlockSpec(memory_space=pltpu.SMEM)
IN_HBM = pl.BlockSpec(memory_space=pltpu.HBM)


def call(body, outputs, in_specs, args, out_specs=None, scratch=()):
    return pl.pallas_call(
        body,
        out_shape=outputs,
        in_specs=in_specs,
        out_specs=jax.tree.map(lambda _: IN_VMEM, outputs) if out_specs is None else out_specs,
        scratch_shapes=scratch,
        compiler_params=pltpu.CompilerParams(vmem_limit_bytes=24 * 1024 * 1024),
    )(*args)


def block(rows, width, dtype=jnp.float32):
    return jax.ShapeDtypeStruct((rows, width), dtype)


def lanes_of(index):
    return slice(index * LANES, (index + 1) * LANES)


def exchange(array, core, masks):
    count = lax.axis_size(AXES)
    route = [(place, place ^ masks[0 if place & core == 0 else 1]) for place in range(count)]
    return lax.ppermute(array, AXES, route)


def chosen_mask(place, core, masks):
    return jnp.where(place & core == 0, masks[0], masks[1])


def three_parts(values):
    high = values.astype(jnp.bfloat16)
    rest = values - high.astype(jnp.float32)
    middle = rest.astype(jnp.bfloat16)
    low = (rest - middle.astype(jnp.float32)).astype(jnp.bfloat16)
    return high, middle, low


def exact_dot(values, table):
    total = None
    for piece in three_parts(values):
        product = jnp.dot(piece, table, preferred_element_type=jnp.float32)
        total = product if total is None else total + product
    return total


def sign_of(left, right):
    parity = left & right
    for shift in (4, 2, 1):
        parity = parity ^ (parity >> shift)
    return (1 - 2 * (parity & 1)).astype(jnp.float32)


def mix(parts):
    left = lax.broadcasted_iota(jnp.int32, (LANES, LANES), 0)
    right = lax.broadcasted_iota(jnp.int32, (LANES, LANES), 1)
    table = sign_of(left, right).astype(jnp.bfloat16)
    parts = list(parts)
    span = 1
    while span < len(parts):
        for index in range(len(parts)):
            if index & span == 0:
                first, second = parts[index], parts[index | span]
                parts[index], parts[index | span] = first + second, first - second
        span *= 2
    total = exact_dot(jnp.concatenate(parts, axis=0), table)
    rows = parts[0].shape[0]
    return [total[index * rows : (index + 1) * rows] for index in range(len(parts))]


def own_kernel(scaling, core, place_ref, slab_ref, flips_ref, out_ref):
    columns = out_ref.shape[0]
    top = jnp.where(place_ref[0] & core == 0, 0, columns)
    for index in range(flips_ref.shape[0]):
        sign = jnp.where(flips_ref[index : index + 1, :] == 0, scaling, -scaling)
        rows = pl.ds(pl.multiple_of(top, ROWS), columns)
        out_ref[:, lanes_of(index)] = slab_ref[rows, lanes_of(index)] * sign


def split_kernel(scaling, core, place_ref, own_ref, other_ref, flips_ref, offset_ref, *out_refs):
    chunk_refs, spread_ref = out_refs[:-1], out_refs[-1]
    spread_ref[...] = jnp.concatenate([offset_ref[...]] * (LANES // offset_ref.shape[1]), axis=1)
    columns = own_ref.shape[0]
    on_first = place_ref[0] & core == 0
    top = jnp.where(on_first, 0, columns)
    turn = jnp.where(on_first, 1.0, -1.0)
    for index in range(flips_ref.shape[0]):
        here = lanes_of(index)
        sign = jnp.where(flips_ref[index : index + 1, :] == 0, scaling, -scaling)
        for number, chunk_ref in enumerate(chunk_refs):
            own = own_ref[number * ROWS : (number + 1) * ROWS, here]
            other = other_ref[pl.ds(pl.multiple_of(top + number * ROWS, ROWS), ROWS), here] * sign
            chunk_ref[:ROWS, here] = own + other
            chunk_ref[ROWS:, here] = (own - other) * turn


def tile_kernel(core, place_ref, offset_ref, other_offset_ref, tile_ref):
    samples = offset_ref.shape[1]
    own = jnp.concatenate([offset_ref[...]] * (LANES // samples), axis=1)
    lane = lax.broadcasted_iota(jnp.int32, (1, LANES), 1)
    own_first = jnp.where(place_ref[0] & core == 0, 0, 1)
    tile = jnp.where(lane // samples % 2 == own_first, own, other_offset_ref[...])
    tile_ref[...] = jnp.broadcast_to(tile.astype(jnp.float32), tile_ref.shape)


def ride_kernel(core, masks, place_ref, own_ref, other_ref, tile_ref, out_ref):
    width = own_ref.shape[1]
    factor = jnp.where(place_ref[0] & chosen_mask(place_ref[0], core, masks) == 0, 1.0, -1.0)
    out_ref[:, :width] = own_ref[...] * factor + other_ref[...]
    for row in range(0, own_ref.shape[0], ROWS):
        out_ref[row : row + ROWS, width:] = tile_ref[...]


def step_kernel(core, masks, place_ref, own_ref, other_ref, out_ref):
    factor = jnp.where(place_ref[0] & chosen_mask(place_ref[0], core, masks) == 0, 1.0, -1.0)
    width = out_ref.shape[1]
    out_ref[...] = own_ref[:, :width] * factor + other_ref[:, :width]


def pick(core, samples, masks, place_ref, tile_ref, chunk_ref, other_ref):
    lane = lax.broadcasted_iota(jnp.int32, (1, LANES), 1)
    place_in = lax.broadcasted_iota(jnp.int32, (LANES, LANES), 0)
    own_chip = lane < 2 * samples
    partner = other_ref[0:1, other_ref.shape[1] - LANES :]
    offsets = jnp.where(own_chip, tile_ref[0:1, :], partner).astype(jnp.int32)
    signs = sign_of(place_in, offsets % LANES).astype(jnp.bfloat16)
    side = jnp.where(place_ref[0] & chosen_mask(place_ref[0], core, masks) == 0, 1.0, -1.0)
    slices = chunk_ref.shape[1] // LANES
    rows = chunk_ref.shape[0]
    stacked = jnp.concatenate([chunk_ref[:, lanes_of(index)] for index in range(slices)], axis=0)
    found = exact_dot(stacked, signs)
    share = found[:rows]
    for index in range(1, slices):
        share = share + found[index * rows : (index + 1) * rows] * sign_of(offsets // LANES, index)
    share = jnp.where(lane // samples % 2 == 0, share[:ROWS], share[ROWS:])
    return share * jnp.where(own_chip, side, 1.0)


def pick_all_kernel(core, samples, masks, place_ref, tile_ref, chunk_ref, other_ref, second_ref, second_other_ref, out_ref, token_ref):
    token_ref[...] = jnp.zeros_like(token_ref)
    late = pick(core, samples, masks[0], place_ref, tile_ref, chunk_ref, other_ref)
    early = pick(core, samples, masks[1], place_ref, tile_ref, second_ref, second_other_ref)
    lane = lax.broadcasted_iota(jnp.int32, late.shape, 1)
    tile = jnp.where(lane < LANES // 2, late, pltpu.roll(early, LANES // 2, 1))
    for place in range(out_ref.shape[0]):
        out_ref[place] = tile


def gram_kernel(core, all_masks, place_ref, shares_ref, after_ref, gram_ref, sketch_ref):
    count, rows, _ = shares_ref.shape
    samples = sketch_ref.shape[0]
    width, half = 2 * samples, LANES // 2
    lane = lax.broadcasted_iota(jnp.int32, (rows, LANES), 1)

    def of_core(place, second):
        first, last = (shares_ref[place ^ masks[second]] for masks in all_masks)
        return shares_ref[place] + pltpu.roll(jnp.where(lane < half, first, last), LANES - width, 1)

    def moved(values, start):
        return pltpu.roll(values, start, 1) if start % LANES else values

    chips = [place for place in range(count) if place & core == 0]
    wraps = []
    for wrap in range(0, len(chips), LANES // width):
        rows_of_all = []
        for second in range(2):
            parts = [of_core(chip | core * second, second) for chip in chips[wrap : wrap + LANES // width]]
            for chunk in range(2):
                joined = moved(parts[0], chunk * half)
                for number in range(1, len(parts)):
                    here = moved(parts[number], (number * width + chunk * half) % LANES)
                    joined = jnp.where(lane >= number * width, here, joined)
                rows_of_all.append(joined)
        wraps.append(jnp.concatenate(rows_of_all, axis=0))
    sketch = jnp.concatenate(wraps, axis=1)
    product = functools.partial(
        lax.dot_general,
        dimension_numbers=(((1,), (1,)), ((), ())),
        precision=lax.Precision.HIGHEST,
        preferred_element_type=jnp.float32,
    )
    gram_ref[...] = product(sketch, sketch) * (1.0 / (count * samples))
    chip = place_ref[0] & ~core
    own = []
    for second in range(2):
        part = of_core(chip | core * second, second)
        own += [part, moved(part, half)]
    start = jnp.where(place_ref[0] & core == 0, 0, samples)
    row = lax.broadcasted_iota(jnp.int32, (samples, LANES), 0)
    spot = lax.broadcasted_iota(jnp.int32, (samples, LANES), 1)
    sketch_ref[...] = product(jnp.where(spot == row + start, 1.0, 0.0), jnp.concatenate(own, axis=0))


def last_kernel(core, masks, place_ref, own_ref, other_ref, after_ref, keep_ref, send_ref):
    on_first = place_ref[0] & core == 0
    factor = jnp.where(place_ref[0] & chosen_mask(place_ref[0], core, masks) == 0, 1.0, -1.0)
    for out_ref, top in ((keep_ref, jnp.where(on_first, 0, ROWS)), (send_ref, jnp.where(on_first, ROWS, 0))):
        rows = pl.ds(pl.multiple_of(top, ROWS), ROWS)
        slices = out_ref.shape[1] // LANES
        parts = [
            own_ref[rows, lanes_of(index)] * factor + other_ref[rows, lanes_of(index)] for index in range(slices)
        ]
        for index, part in enumerate(mix(parts)):
            out_ref[:, lanes_of(index)] = part


def join_kernel(core, place_ref, *refs):
    block_refs, (whole_ref, token_ref, sems) = refs[:-3], refs[-3:]
    token_ref[...] = jnp.zeros_like(token_ref)
    on_first = place_ref[0] & core == 0
    half = whole_ref.shape[0] // 2
    tops = []
    for kept in (True, False):
        base = jnp.where(on_first, 0, half) if kept else jnp.where(on_first, half, 0)
        tops += [base + row for row in range(0, half, ROWS)]
    copies = [
        pltpu.make_async_copy(
            block_ref, whole_ref.at[pl.ds(pl.multiple_of(top, ROWS), ROWS)], sems.at[number]
        )
        for number, (block_ref, top) in enumerate(zip(block_refs, tops))
    ]
    for copy in copies:
        copy.start()
    for copy in copies:
        copy.wait()


def local_any(matrix_slab, sign_flips, sample_offset):
    columns, local_rows = matrix_slab.shape
    count = lax.axis_size(AXES)
    samples = sample_offset.shape[0]
    numbers = jnp.arange(local_rows, dtype=jnp.int32)

    def table(order):
        common = numbers[:order, None] & numbers[None, :order]
        return (1 - 2 * (lax.population_count(common) & 1)).astype(jnp.float32)

    signs = (1 - 2 * sign_flips).astype(jnp.float32) * jnp.float32(1.0 / math.sqrt(local_rows * count))
    outer = local_rows // LANES
    shaped = (matrix_slab * signs[None, :]).reshape(columns, outer, LANES)
    shaped = jnp.einsum("cak,kz->caz", shaped, table(LANES), precision=lax.Precision.HIGHEST)
    shaped = jnp.einsum("cak,az->czk", shaped, table(outer), precision=lax.Precision.HIGHEST)
    current = shaped.reshape(columns, local_rows)
    for bit in range(count.bit_length() - 1):
        other = exchange(current, 1, (1 << bit, 1 << bit))
        lower = lax.axis_index(AXES) & 1 << bit == 0
        current = jnp.where(lower, current + other, other - current)
    sketch = jnp.take(current, sample_offset, axis=1)
    gram = jnp.dot(sketch, sketch.T, precision=lax.Precision.HIGHEST)
    return (current, sketch, lax.psum(gram, AXES) / jnp.float32(samples * count))


def local(matrix_slab, sign_flips, sample_offset):
    columns, local_rows = matrix_slab.shape
    grp_bits = lax.axis_size("grp").bit_length() - 1
    dev_bits = lax.axis_size("dev").bit_length() - 1
    count = lax.axis_size(AXES)
    samples = sample_offset.shape[0]
    if (grp_bits, dev_bits, columns, samples) != (2, 3, 4 * ROWS, 2 * ROWS):
        return local_any(matrix_slab, sign_flips, sample_offset)
    place = lax.axis_index(AXES).astype(jnp.int32).reshape(1)
    flips = sign_flips.reshape(local_rows // LANES, LANES)
    offsets = sample_offset.reshape(1, samples)
    y, z_low, z_high, core, x = (1 << bit for bit in range(dev_bits + grp_bits))
    scaling = 1.0 / math.sqrt(local_rows * count)
    across = (core, core)
    orders = [
        [(y, z_low), (x, z_high), (z_high, y), (z_low, x)],
        [(x, z_high), (y, z_low), (z_low, x), (z_high, y)],
    ]

    other = exchange(matrix_slab, core, across)
    other_flips = exchange(flips, core, across)
    other_offsets = exchange(offsets, core, across)
    own = call(
        functools.partial(own_kernel, scaling, core),
        block(columns // 2, local_rows),
        [IN_SMEM, IN_VMEM, IN_VMEM],
        [place, matrix_slab, flips],
    )
    chunk = block(2 * ROWS, local_rows)
    *chunks, spread = call(
        functools.partial(split_kernel, scaling, core),
        [chunk, chunk, block(1, LANES, jnp.int32)],
        [IN_SMEM] + [IN_VMEM] * 4,
        [place, own, other, other_flips, other_offsets],
    )
    tile = call(
        functools.partial(tile_kernel, core),
        block(ROWS, LANES),
        [IN_SMEM] + [IN_VMEM] * 2,
        [place, offsets, spread],
    )
    ridden, thirds = [], []
    for current, order in zip(chunks, orders):
        current = call(
            functools.partial(step_kernel, core, order[0]),
            chunk,
            [IN_SMEM] + [IN_VMEM] * 2,
            [place, current, exchange(current, core, order[0])],
        )
        current = call(
            functools.partial(ride_kernel, core, order[1]),
            block(2 * ROWS, local_rows + LANES),
            [IN_SMEM] + [IN_VMEM] * 3,
            [place, current, exchange(current, core, order[1]), tile],
        )
        partner = exchange(current, core, order[2])
        ridden.append(partner)
        thirds.append(
            call(
                functools.partial(step_kernel, core, order[2]),
                chunk,
                [IN_SMEM] + [IN_VMEM] * 2,
                [place, current, partner],
            )
        )
    first, second = thirds
    last_masks = [order[3] for order in orders]
    shares, picked = call(
        functools.partial(pick_all_kernel, core, samples, last_masks),
        [jax.ShapeDtypeStruct((count, ROWS, LANES), jnp.float32), block(ROWS, LANES)],
        [IN_SMEM] + [IN_VMEM] * 5,
        [place, tile, first, ridden[1], second, ridden[0]],
    )
    lasts = [
        call(
            functools.partial(last_kernel, core, masks),
            [block(ROWS, local_rows)] * 2,
            [IN_SMEM] + [IN_VMEM] * 3,
            [place, current, exchange(current, core, masks), picked],
        )
        for current, masks in zip((first, second), last_masks)
    ]
    kept = [keep for keep, _ in lasts]
    back = [exchange(send, core, across) for _, send in lasts]
    transformed, token = call(
        functools.partial(join_kernel, core),
        [block(columns, local_rows), block(ROWS, LANES)],
        [IN_SMEM] + [IN_VMEM] * 4,
        [place, *kept, *back],
        out_specs=[IN_HBM, IN_VMEM],
        scratch=[pltpu.SemaphoreType.DMA((4,))],
    )
    gram, sketch = call(
        functools.partial(gram_kernel, core, last_masks),
        [block(columns, columns), block(samples, columns)],
        [IN_SMEM, IN_VMEM, IN_VMEM],
        [place, lax.all_to_all(shares, AXES, 0, 0, tiled=True), token],
    )
    return (transformed, sketch.T, gram)


def solution(mesh):
    return jax.shard_map(
        local,
        mesh=mesh,
        in_specs=(P(None, AXES), P(AXES), P(AXES)),
        out_specs=(P(None, AXES), P(None, AXES), P()),
        check_vma=False,
    )
```
